128 devices in a mesh: dp: 4 (over z_hi, core), section: 8 (over z_lo, x), tensor: 4 (over y).
Axes of the slice: x: 4, y: 4, z: 4 (z_hi: 2, z_lo: 2; z = z_hi * 2 + z_lo), core: 2. Of those that a mesh axis runs over, the one named last changes fastest.
Arguments:
- queries: bfloat16 [8, 8192, 4096], P('section', 'dp', 'tensor'), may hold values from -68 to 68
- cotangent: bfloat16 [8, 8192, 4096], P('section', 'dp', 'tensor'), may hold values from -6 to 6
- vision: bfloat16 [2048, 8192], P(('dp', 'section', 'tensor')), may hold values from -6 to 6
- kv_weight: bfloat16 [8, 8192, 4, 256], P('section', 'dp', 'tensor'), may hold values from -0.0625 to 0.0625
- visible_tiles: int32 [4, 16, 8], P('dp'), may hold values from 0 to 1, as said below
- image_count: int32 [4], P('dp'), may hold values from 1 to 2
Outputs:
- context: bfloat16 [8, 8192, 4096], P('section', 'dp', 'tensor')
- grad_queries: bfloat16 [8, 8192, 4096], P('section', 'dp', 'tensor')
- grad_vision: float32 [2048, 8192], P(('dp', 'section', 'tensor'))
- grad_kv_weight: float32 [8, 8192, 4, 256], P('section', 'dp', 'tensor')
The draws below stay inside these ranges and needn't reach their ends.
Inputs may be any that keep to these rules, and one draw needn't show every extreme that they name: `visible_tiles`: in every document one whole block of 128 text tokens sees no tile.
All inputs are finite; a program needn't handle non-finite values.
Results may differ from the reference program's by a relative error of at most 0.017.
The reference program's roundings to bfloat16 on the way (of `key_value`, `probs_low`, `score_grad` and `kv_grad`) count: a program that leaves them out, or rounds other values in their place, can miss the bound.
Values may be sent and summed in bfloat16 or wider, within the bound.
No kernel may reach another device: no remote copies, remote signals or barrier semaphores. Data moves between devices by JAX's collectives and lax.ppermute only.
A program may use at most 192 MiB of HBM per device.

```python
import jax
import jax.numpy as jnp
from jax import lax

D = 8192
HEADS = 32
KV = 4
HD = 128
IMAGES = 2
TILES = 4
TEXT_BLOCK = 128
TEXT_LEN = 2048
TILE_ROWS = 64
ROW_BLOCK = 512
LAYERS = 8
TOKENS = 8192
VIS = 512
VISION = 2048
BLOCKS = 16
N_DP = 4


def draw_queries(key, part):
    key = jax.random.fold_in(key, 11)
    key_base = jax.random.fold_in(key, 0)
    shape = (LAYERS, TOKENS, HEADS * HD)
    values = jnp.clip(jax.random.normal(key_base, shape, jnp.float32), -6.0, 6.0)
    return values.astype(jnp.bfloat16)


def draw_visible_tiles(key, part):
    key = jax.random.fold_in(key, 23)
    key_marks, key_block = jax.random.split(key, 2)
    shape = (N_DP, BLOCKS, IMAGES * TILES)
    marks = (jax.random.randint(key_marks, shape, 0, 4) < 3).astype(jnp.int32)
    empty_block = jax.random.randint(key_block, (N_DP, 1, 1), 0, BLOCKS)
    block_index = jnp.arange(BLOCKS, dtype=jnp.int32)[None, :, None]
    return jnp.where(block_index == empty_block, jnp.zeros_like(marks), marks).astype(jnp.int32)


def set_ends(values, key, smallest, largest):
    spot = [jax.random.randint(jax.random.fold_in(key, axis), (), 0, length) for axis, length in enumerate(values.shape)]
    longest = values.shape.index(max(values.shape))
    beside = spot[:longest] + [(spot[longest] + 1) % values.shape[longest]] + spot[longest + 1:]
    return values.at[tuple(spot)].set(smallest).at[tuple(beside)].set(largest)


def block_levels(rng, dims, pieces, smallest, top_value):
    loudness = 1.0
    for axis_at, blocks in pieces:
        heights = jax.random.uniform(jax.random.fold_in(jax.random.fold_in(rng, 6), axis_at), (blocks,), jnp.float32, smallest / len(pieces), top_value / len(pieces))
        loudness = loudness * jnp.repeat(jnp.exp(heights), dims[axis_at] // blocks).reshape((-1,) + (1,) * (len(dims) - 1 - axis_at))
    return loudness


def normal_values(stream_key, extent, width, bound, cuts=(), held_as=jnp.bfloat16):
    result = jax.random.normal(stream_key, extent, jnp.float32) * width
    if len(cuts) > 0:
        result = block_levels(stream_key, extent, cuts, -0.22, 0.18) * result
    return jnp.clip(result, min=-bound, max=bound).astype(held_as)


def setup_inputs(seed: int = 0) -> dict:
    keys = jax.random.split(jax.random.key(seed), 7)
    queries = draw_queries(jax.random.fold_in(keys[6], 71), 0)
    cotangent = normal_values(keys[1], (LAYERS, TOKENS, HEADS * HD), 1.0, 6.0, ((0, 8), (1, 4), (2, 4)))
    vision = normal_values(keys[2], (VISION, D), 1.0, 6.0, ((0, 128),))
    kv_weight = normal_values(keys[3], (LAYERS, D, KV, 2 * HD), D ** -0.5, 0.0625, ((0, 8), (1, 4), (2, 4)))
    visible_tiles = draw_visible_tiles(jax.random.fold_in(keys[6], 71), 0)
    image_count = set_ends(jax.random.randint(keys[5], (N_DP,), 1, IMAGES + 1), jax.random.fold_in(keys[5], 1), 1, IMAGES).astype(jnp.int32)
    return {"queries": queries, "cotangent": cotangent, "vision": vision, "kv_weight": kv_weight, "visible_tiles": visible_tiles, "image_count": image_count}


def build_visible(tile_mask, image_total):
    key_tile = jnp.repeat(tile_mask, TILE_ROWS, axis=1)
    row_tile = jnp.repeat(key_tile, TEXT_BLOCK, axis=0)
    key_image = jnp.arange(row_tile.shape[1], dtype=jnp.int32) // (TILES * TILE_ROWS)
    return (row_tile == 1) & (key_image < image_total)[None, :]


def attend_block(query_part, cot_part, key_rows, value_rows, visible):
    score_scale = HD ** -0.5
    wide = jnp.float32
    scores = jnp.einsum('rkgd,jkd->rkgj', query_part.astype(wide), key_rows.astype(wide)) * score_scale
    seen = visible[:, None, None, :]
    any_seen = jnp.any(visible, axis=-1)[:, None, None, None]
    peak = jnp.max(jnp.where(seen, scores, -jnp.inf), axis=-1, keepdims=True)
    peak = jnp.where(any_seen, peak, jnp.zeros_like(peak))
    expon = jnp.where(seen, jnp.exp(scores - peak), jnp.zeros_like(scores))
    total = jnp.sum(expon, axis=-1, keepdims=True)
    total = jnp.where(any_seen, total, jnp.ones_like(total))
    probs = expon / total
    probs_low = probs.astype(jnp.bfloat16)
    context = jnp.einsum('rkgj,jkd->rkgd', probs_low.astype(wide), value_rows.astype(wide)).astype(jnp.bfloat16)
    prob_grad = jnp.einsum('rkgd,jkd->rkgj', cot_part.astype(wide), value_rows.astype(wide))
    delta = jnp.sum(probs * prob_grad, axis=-1, keepdims=True)
    score_grad = (probs * (prob_grad - delta) * score_scale).astype(jnp.bfloat16)
    query_grad = jnp.einsum('rkgj,jkd->rkgd', score_grad.astype(wide), key_rows.astype(wide)).astype(jnp.bfloat16)
    key_grad = jnp.einsum('rkgj,rkgd->jkd', score_grad.astype(wide), query_part.astype(wide))
    value_grad = jnp.einsum('rkgj,rkgd->jkd', probs_low.astype(wide), cot_part.astype(wide))
    return context, query_grad, key_grad, value_grad


def doc_layer(query_doc, cot_doc, image_rows, layer_weight, tile_mask, image_total):
    group_size = HEADS // KV
    block_count = TEXT_LEN // ROW_BLOCK
    key_value = jnp.dot(image_rows, layer_weight.reshape(D, KV * 2 * HD), preferred_element_type=jnp.float32)
    key_value = key_value.astype(jnp.bfloat16).reshape(VIS, KV, 2 * HD)
    key_rows = key_value[:, :, :HD]
    value_rows = key_value[:, :, HD:]
    visible = build_visible(tile_mask, image_total).reshape(block_count, ROW_BLOCK, VIS)
    query_blocks = query_doc.reshape(block_count, ROW_BLOCK, KV, group_size, HD)
    cot_blocks = cot_doc.reshape(block_count, ROW_BLOCK, KV, group_size, HD)

    def block_step(totals, slices):
        context, query_grad, key_grad, value_grad = attend_block(slices[0], slices[1], key_rows, value_rows, slices[2])
        return (totals[0] + key_grad, totals[1] + value_grad), (context, query_grad)

    empty_grads = jnp.zeros((VIS, KV, HD), jnp.float32)
    (key_grad, value_grad), (context, query_grad) = lax.scan(block_step, (empty_grads, empty_grads), (query_blocks, cot_blocks, visible))
    kv_grad = jnp.concatenate([key_grad, value_grad], axis=-1).astype(jnp.bfloat16)
    return context.reshape(TEXT_LEN, HEADS * HD), query_grad.reshape(TEXT_LEN, HEADS * HD), kv_grad


def reference(queries, cotangent, vision, kv_weight, visible_tiles, image_count):
    image_docs = vision.reshape(N_DP, VIS, D)

    def per_layer(vision_total, slices):
        query_layer, cot_layer, layer_weight = slices

        def per_doc(parts):
            return doc_layer(parts[0], parts[1], parts[2], layer_weight, parts[3], parts[4])

        context, query_grad, kv_grad = lax.map(per_doc, (query_layer.reshape(N_DP, TEXT_LEN, HEADS * HD), cot_layer.reshape(N_DP, TEXT_LEN, HEADS * HD), image_docs, visible_tiles, image_count))
        grad_wide = kv_grad.astype(jnp.float32)
        vision_total = vision_total + jnp.einsum('gvkc,dkc->gvd', grad_wide, layer_weight.astype(jnp.float32))
        weight_grad = jnp.einsum('gvd,gvkc->dkc', image_docs.astype(jnp.float32), grad_wide)
        return vision_total, (context.reshape(TOKENS, HEADS * HD), query_grad.reshape(TOKENS, HEADS * HD), weight_grad)

    start_total = jnp.zeros((N_DP, VIS, D), jnp.float32)
    vision_total, (context, grad_queries, grad_kv_weight) = lax.scan(per_layer, start_total, (queries, cotangent, kv_weight))
    return context, grad_queries, vision_total.reshape(VISION, D), grad_kv_weight
```

```python
import jax, jax.numpy as jnp
from jax import lax
from jax.experimental import pallas as pl
from jax.experimental.pallas import tpu as pltpu
from jax.sharding import Mesh
from jax.sharding import PartitionSpec as P

HD=128; GROUP=8; TILES=4; TEXT_BLOCK=128; SEC=8
HIDDEN=-1e30
LOG2E=1.4426950408889634

def attend_kernel(tiles_ref, count_ref, q_ref, cot_ref, kv_ref, ctx_ref, dq_ref, dkv_ref, key_t, value_t, dkey, dvalue):
    block = pl.program_id(0)
    scale = HD ** (-0.5)
    wide = jnp.float32
    low = jnp.bfloat16

    @pl.when(block == 0)
    def _():
        key_t[...] = kv_ref[:, :HD].astype(wide).T.astype(low)
        value_t[...] = kv_ref[:, HD:].astype(wide).T.astype(low)
        dkey[...] = jnp.zeros_like(dkey)
        dvalue[...] = jnp.zeros_like(dvalue)

    seen = [(tiles_ref[block, t] == 1) & (t // TILES < count_ref[0]) for t in range(SEC)]
    any_seen = seen[0]
    for t in range(1, SEC):
        any_seen = any_seen | seen[t]

    @pl.when(jnp.logical_not(any_seen))
    def _():
        ctx_ref[...] = jnp.zeros_like(ctx_ref)
        dq_ref[...] = jnp.zeros_like(dq_ref)

    @pl.when(any_seen)
    def _():
        bias = [jnp.where(s, 0.0, HIDDEN).astype(wide) for s in seen]
        rows = kv_ref.shape[0]
        for pair in range(GROUP // 2):
            at = pair * 2 * HD
            q2 = jnp.concatenate([q_ref[:, at:at + HD], q_ref[:, at + HD:at + 2 * HD]], axis=0)
            g2 = jnp.concatenate([cot_ref[:, at:at + HD], cot_ref[:, at + HD:at + 2 * HD]], axis=0)
            scores = lax.dot_general(kv_ref[:, :HD], q2, (((1,), (1,)), ((), ())), preferred_element_type=wide)
            scores = jnp.concatenate([scores[r * 16:r * 16 + 16] + bias[r % SEC] for r in range(rows // 16)], axis=0)
            peak = jnp.max(scores, axis=0, keepdims=True)
            expon = jnp.exp2((scores - peak) * (scale * LOG2E))
            probs = expon * (1.0 / jnp.sum(expon, axis=0, keepdims=True))
            probs_low = probs.astype(low)
            ctx = jnp.dot(value_t[...], probs_low, preferred_element_type=wide).T.astype(low)
            ctx_ref[:, at:at + HD] = ctx[:TEXT_BLOCK]
            ctx_ref[:, at + HD:at + 2 * HD] = ctx[TEXT_BLOCK:]
            prob_grad = lax.dot_general(kv_ref[:, HD:], g2, (((1,), (1,)), ((), ())), preferred_element_type=wide)
            delta = jnp.sum(probs * prob_grad, axis=0, keepdims=True)
            score_grad = (probs * ((prob_grad - delta) * scale)).astype(low)
            dq = jnp.dot(key_t[...], score_grad, preferred_element_type=wide).T.astype(low)
            dq_ref[:, at:at + HD] = dq[:TEXT_BLOCK]
            dq_ref[:, at + HD:at + 2 * HD] = dq[TEXT_BLOCK:]
            dkey[...] += jnp.dot(score_grad, q2, preferred_element_type=wide)
            dvalue[...] += jnp.dot(probs_low, g2, preferred_element_type=wide)

    @pl.when(block == pl.num_programs(0) - 1)
    def _():
        dkv_ref[:, :HD] = dkey[...].astype(low)
        dkv_ref[:, HD:] = dvalue[...].astype(low)


def attend(tiles, count, queries, cot, kv):
    text, width = queries.shape
    blocks = text // TEXT_BLOCK
    vis = kv.shape[0]
    wide = pl.BlockSpec((TEXT_BLOCK, width), lambda b: (b, 0))
    whole = pl.BlockSpec((vis, 2 * HD), lambda b: (0, 0))
    flops = 12 * text * width * vis
    return pl.pallas_call(
        attend_kernel,
        grid=(blocks,),
        in_specs=[pl.BlockSpec(memory_space=pltpu.SMEM), pl.BlockSpec(memory_space=pltpu.SMEM), wide, wide, whole],
        out_specs=[wide, wide, whole],
        out_shape=[jax.ShapeDtypeStruct(queries.shape, jnp.bfloat16), jax.ShapeDtypeStruct(queries.shape, jnp.bfloat16),
                   jax.ShapeDtypeStruct(kv.shape, jnp.bfloat16)],
        scratch_shapes=[pltpu.VMEM((HD, vis), jnp.bfloat16), pltpu.VMEM((HD, vis), jnp.bfloat16),
                        pltpu.VMEM((vis, HD), jnp.float32), pltpu.VMEM((vis, HD), jnp.float32)],
        compiler_params=pltpu.CompilerParams(vmem_limit_bytes=48 * 1024 * 1024),
        cost_estimate=pl.CostEstimate(flops=flops, bytes_accessed=4 * text * width * 2, transcendentals=text * width // HD * vis),
    )(tiles, count, queries, cot, kv)


DP = ("zh", "co")
SECTION = ("zl", "x")
KV_COLS = 2 * HD


def shift(array, axis, size, step):
    return lax.ppermute(array, axis, [(i, (i + step) % size) for i in range(size)])


def ring_y(array):
    below = shift(array, "y", 4, 1)
    above = shift(array, "y", 4, -1)
    half = array.shape[0] // 2
    first = shift(below[:half], "y", 4, 1)
    second = shift(above[half:], "y", 4, -1)
    return [array, below, above, jnp.concatenate([first, second], axis=0)]


RING = (0, -1, 1, 2)


def local(queries, cotangent, vision, kv_weight, visible_tiles, image_count):
    wide, low = jnp.float32, jnp.bfloat16
    rows, width = vision.shape
    depth = width // 4
    sections = 8
    y = lax.axis_index("y")
    zh = lax.axis_index("zh")
    co = lax.axis_index("co")

    weight = kv_weight.reshape(depth, KV_COLS)
    weights = ring_y(weight)

    own = vision.reshape(rows, 4, depth).transpose(1, 0, 2)
    own = lax.all_to_all(own, DP, 0, 0, tiled=True)
    features = lax.all_to_all(
        jnp.broadcast_to(own[None], (sections,) + own.shape), SECTION, 0, 0, tiled=True
    ).reshape(sections * 4 * rows, depth)

    parts = [jnp.dot(features, w, preferred_element_type=wide).reshape(sections, 4, rows, KV_COLS) for w in weights]
    part = jnp.stack(parts).reshape(4, sections, 2, 2, rows, KV_COLS)
    keep = lax.dynamic_index_in_dim(part, co, 3, keepdims=False)
    away = lax.dynamic_index_in_dim(part, 1 - co, 3, keepdims=False)
    part = keep + shift(away, "co", 2, 1)
    keep = lax.dynamic_index_in_dim(part, zh, 2, keepdims=False)
    away = lax.dynamic_index_in_dim(part, 1 - zh, 2, keepdims=False)
    key_value = (keep + shift(away, "zh", 2, 1)).astype(low)
    pieces = [key_value[j] if step == 0 else shift(key_value[j], "y", 4, step) for j, step in enumerate(RING)]
    kv = jnp.stack(pieces).reshape(4 * sections * rows, KV_COLS)

    features, kv = lax.optimization_barrier((features, kv))
    feature_ring = ring_y(features)

    context, grad_queries, kv_grad = attend(visible_tiles[0], image_count, queries[0], cotangent[0], kv)

    kv_grad = kv_grad.reshape(4, sections, rows, KV_COLS)
    back = [kv_grad[j] if step == 0 else shift(kv_grad[j], "y", 4, -step) for j, step in enumerate(RING)]
    heads = jnp.stack(back)

    def over_dp(block):
        other = shift(block, "zh", 2, 1)
        low_block = jnp.where(zh == 0, block, other)
        high_block = jnp.where(zh == 0, other, block)
        pair = jnp.stack([low_block, high_block])
        pair_other = shift(pair, "co", 2, 1)
        low_pair = jnp.where(co == 0, pair, pair_other)
        high_pair = jnp.where(co == 0, pair_other, pair)
        return jnp.stack([low_pair, high_pair], axis=1)

    all_heads = over_dp(heads).reshape(4, 4, sections, rows, KV_COLS)
    all_heads = all_heads.transpose(1, 2, 0, 3, 4).reshape(4, sections * 4 * rows, KV_COLS)
    vision_part = sum(
        lax.dot_general(all_heads[j], weights[j], (((1,), (1,)), ((), ())), preferred_element_type=wide)
        for j in range(4)
    )
    vision_part = vision_part.astype(low).reshape(sections, 4 * rows, depth)
    vision_part = lax.all_to_all(vision_part, SECTION, 0, 0, tiled=True)
    vision_part = jnp.sum(vision_part.astype(wide), axis=0).astype(low).reshape(4, rows, depth)
    vision_part = lax.all_to_all(vision_part, DP, 0, 0, tiled=True)
    grad_vision = vision_part.transpose(1, 0, 2).reshape(rows, width).astype(wide)

    own_head = over_dp(kv_grad).reshape(4, 4, sections, rows, KV_COLS)
    own_head = own_head.transpose(1, 2, 0, 3, 4).reshape(4, sections * 4 * rows, KV_COLS)
    match = (0, 2, 1, 3)
    grad_weight = sum(
        lax.dot_general(feature_ring[match[j]], own_head[j], (((0,), (0,)), ((), ())), preferred_element_type=wide)
        for j in range(4)
    )
    return (
        context[None],
        grad_queries[None],
        grad_vision,
        grad_weight.reshape(1, depth, 1, KV_COLS),
    )


def solution(mesh):
    fine = Mesh(mesh.devices.reshape(2, 2, 2, 4, 4), ("zh", "co", "zl", "x", "y"))
    return jax.shard_map(
        local,
        mesh=fine,
        in_specs=(
            P(SECTION, DP, "y"),
            P(SECTION, DP, "y"),
            P(DP + SECTION + ("y",), None),
            P(SECTION, DP, "y", None),
            P(DP, None, None),
            P(DP),
        ),
        out_specs=(
            P(SECTION, DP, "y"),
            P(SECTION, DP, "y"),
            P(DP + SECTION + ("y",), None),
            P(SECTION, DP, "y", None),
        ),
        check_vma=False,
    )
```
